32 devices in a mesh: gx: 2 (over y), gy: 4 (over x, core), gz: 4 (over z).
Axes of the slice: x: 2, y: 2, z: 4, core: 2. Of those that a mesh axis runs over, the one named last changes fastest.
Arguments:
- species: float32 [16, 16, 16, 654], P('gx', 'gy', 'gz'), may hold values from -6 to 6
- counts: int32 [16, 16, 16], P('gx', 'gy', 'gz'), may hold values from 1 to 8, as said below
- assignment: int32 [16, 16, 16], P('gx', 'gy', 'gz'), may hold values from 0 to 7, as said below
- cell_scale: float32 [16, 16, 16], P('gx', 'gy', 'gz'), may hold values from 0.5 to 1
- diffusivity: float32 [654], replicated, may hold values from 0.02 to 0.16
- order_weights: bfloat16 [654, 1536], replicated, may hold values from -0.25 to 0.25
- stoichiometry: bfloat16 [1536, 654], replicated, may hold values from -0.15625 to 0.15625
- rate_factor: float32 [1536], replicated, may hold values from 0.3 to 3
- enthalpy: float32 [654], replicated, may hold values from -4 to 4
Outputs:
- advanced: float32 [16, 16, 16, 654], P('gx', 'gy', 'gz')
- worker_heat: float32 [2, 4, 4], P('gx', 'gy', 'gz')
The draws below stay inside these ranges and needn't reach their ends.
Inputs may be any that keep to these rules, and one draw needn't show every extreme that they name: `counts`: cells with many substeps cluster in one region of the grid. `assignment`: among the 128 cells of each device, exactly 16 are assigned to each device of its gx-gy plane.
All inputs are finite; a program needn't handle non-finite values.
Results may differ from the reference program's by a relative error of at most 0.0025.
Values sent between devices are 32-bit elements; how exact they have to be, the bound alone decides.
A program may use at most 64 MiB of HBM per device.

```python
import math
import jax
import jax.numpy as jnp
from jax import lax

S = 654
R = 1536
CX = 8
CY = 4
CZ = 4
MAXSUB = 8
CELLS = 128
NX = 16
NY = 16
NZ = 16
N_GX = 2
N_GY = 4
N_GZ = 4


def flame_counts(key):
    base_counts = jax.random.randint(jax.random.fold_in(key, 11), (NX, NY, NZ), 1, 3)
    flame_values = jax.random.randint(jax.random.fold_in(key, 12), (NX, NY, NZ), 6, MAXSUB + 1)
    centre = jax.random.randint(jax.random.fold_in(key, 13), (3,), 0, 1024)
    along_x = jnp.arange(NX, dtype=jnp.int32) * 1024 // NX - centre[0]
    along_y = jnp.arange(NY, dtype=jnp.int32) * 1024 // NY - centre[1]
    along_z = jnp.arange(NZ, dtype=jnp.int32) * 1024 // NZ - centre[2]
    radius_sq = (along_x * along_x)[:, None, None] + (along_y * along_y)[None, :, None] + (along_z * along_z)[None, None, :]
    return jnp.where(radius_sq < 360 * 360, flame_values, base_counts).astype(jnp.int32)


def draw_counts(key, part):
    return flame_counts(jax.random.fold_in(key, 101))


def draw_assignment(key, part):
    counts = flame_counts(jax.random.fold_in(key, 101))
    span_x = NX // CX
    span_y = NY // CY
    span_z = NZ // CZ
    cell_count = CX * CY * CZ
    group_size = span_x * span_y
    device_total = span_x * span_y * span_z
    blocks = counts.reshape(span_x, CX, span_y, CY, span_z, CZ).transpose(0, 2, 4, 1, 3, 5).reshape(device_total, cell_count)
    noise_bits = jax.random.randint(jax.random.fold_in(key, 102), (device_total, cell_count), 0, 1 << 30)
    tie_ranks = jnp.argsort(jnp.argsort(noise_bits, axis=1, stable=True), axis=1, stable=True).astype(jnp.int32)
    scores = (MAXSUB - blocks) * cell_count + tie_ranks
    slot_ranks = jnp.argsort(jnp.argsort(scores, axis=1, stable=True), axis=1, stable=True).astype(jnp.int32)
    offsets = jax.random.randint(jax.random.fold_in(key, 103), (device_total, 1), 0, group_size)
    targets = (slot_ranks + offsets) % group_size
    targets = targets.reshape(span_x, span_y, span_z, CX, CY, CZ).transpose(0, 3, 1, 4, 2, 5).reshape(NX, NY, NZ)
    return targets.astype(jnp.int32)


def block_levels(rng, extent, pieces, least, high):
    def one(dim, parts):
        heights = jax.random.uniform(jax.random.fold_in(jax.random.fold_in(rng, 6), dim), (parts,), jnp.float32, least / len(pieces), high / len(pieces))
        return jnp.repeat(jnp.exp(heights), extent[dim] // parts).reshape((-1,) + (1,) * (len(extent) - dim - 1))

    level = one(*pieces[0])
    for cut in pieces[1:]:
        level = level * one(*cut)
    return level


def scatter_about(own_key, extent, deviation, most, shards=(), kind=jnp.bfloat16):
    result = deviation * jax.random.normal(own_key, extent, jnp.float32)
    if shards:
        result = result * block_levels(own_key, extent, shards, -0.22, 0.18)
    return jnp.clip(result, -most, most).astype(kind)


def setup_inputs(seed: int = 0) -> dict:
    splits = jax.random.split(jax.random.key(seed), 10)
    return {
        "species": scatter_about(splits[0], (NX, NY, NZ, S), 1.0, 6.0, ((0, 2), (1, 4), (2, 4)), jnp.float32),
        "counts": draw_counts(jax.random.fold_in(splits[9], 71), 0),
        "assignment": draw_assignment(jax.random.fold_in(splits[9], 71), 0),
        "cell_scale": jnp.clip(0.5 + 0.5 * jax.random.uniform(splits[3], (NX, NY, NZ), jnp.float32) ** block_levels(splits[3], (NX, NY, NZ), ((0, 2), (1, 4), (2, 4)), -0.2, 0.2), 0.5, 1.0),
        "diffusivity": jnp.clip(jnp.exp(jax.random.uniform(splits[4], (S,), jnp.float32, math.log(0.02), math.log(0.16))), 0.02, 0.16),
        "order_weights": scatter_about(splits[5], (S, R), S ** -0.5, 0.25),
        "stoichiometry": scatter_about(splits[6], (R, S), R ** -0.5, 0.15625),
        "rate_factor": jnp.clip(jnp.exp(jax.random.uniform(splits[7], (R,), jnp.float32, math.log(0.3), math.log(3.0))), 0.3, 3.0),
        "enthalpy": scatter_about(splits[8], (S,), 0.3, 4.0, (), jnp.float32),
    }


relax_rate = 0.25


def section(state_now, cell_scale, diffusivity):
    padded = jnp.pad(state_now, ((1, 1), (1, 1), (1, 1), (0, 0)))
    beside_all = padded[2:, 1:-1, 1:-1] + padded[:-2, 1:-1, 1:-1]
    beside_all = beside_all + padded[1:-1, 2:, 1:-1] + padded[1:-1, :-2, 1:-1]
    beside_all = beside_all + padded[1:-1, 1:-1, 2:] + padded[1:-1, 1:-1, :-2]
    return state_now + cell_scale[..., None] * diffusivity * (beside_all - 6.0 * state_now)


def substep(tile_rows, order_wide, stoich_wide, rate_factor):
    rounded = lax.optimization_barrier(tile_rows.astype(jnp.bfloat16))
    activity = jnp.dot(rounded.astype(jnp.float32), order_wide, precision=lax.Precision.HIGHEST)
    rate_values = lax.optimization_barrier((rate_factor * jax.nn.softplus(activity)).astype(jnp.bfloat16))
    change = jnp.dot(rate_values.astype(jnp.float32), stoich_wide, precision=lax.Precision.HIGHEST)
    return tile_rows + relax_rate * (change - tile_rows)


def advance(cell_rows, cell_counts, order_wide, stoich_wide, rate_factor, enthalpy, block_size):
    row_total = cell_rows.shape[0]
    positions = jnp.arange(row_total, dtype=jnp.int32)
    scores = (MAXSUB - cell_counts).astype(jnp.int32) * row_total + positions
    ordering = jnp.argsort(scores, stable=True).astype(jnp.int32)
    sorted_rows = cell_rows[ordering]
    sorted_counts = cell_counts[ordering]
    heat_rows = jnp.zeros((row_total,), jnp.float32)
    for substep_no in range(MAXSUB):
        live_rows = jnp.sum((sorted_counts > substep_no).astype(jnp.int32))
        block_count = (live_rows + block_size - 1) // block_size

        def advance_block(index, carried, substep_no=substep_no):
            rows_now, heat_now = carried
            start = (index * block_size).astype(jnp.int32)
            tile_rows = lax.dynamic_slice_in_dim(rows_now, start, block_size, 0)
            tile_counts = lax.dynamic_slice_in_dim(sorted_counts, start, block_size, 0)
            tile_heat = lax.dynamic_slice_in_dim(heat_now, start, block_size, 0)
            stepped = substep(tile_rows, order_wide, stoich_wide, rate_factor)
            active = tile_counts > substep_no
            released = jnp.sum(enthalpy * (tile_rows - stepped), axis=1)
            tile_heat = tile_heat + jnp.where(active, released, jnp.float32(0.0))
            tile_rows = jnp.where(active[:, None], stepped, tile_rows)
            rows_now = lax.dynamic_update_slice_in_dim(rows_now, tile_rows, start, 0)
            heat_now = lax.dynamic_update_slice_in_dim(heat_now, tile_heat, start, 0)
            return rows_now, heat_now

        sorted_rows, heat_rows = lax.fori_loop(0, block_count, advance_block, (sorted_rows, heat_rows))
    inverse = jnp.zeros((row_total,), jnp.int32).at[ordering].set(positions)
    return sorted_rows[inverse], heat_rows[inverse]


def reference(species, counts, assignment, cell_scale, diffusivity, order_weights, stoichiometry, rate_factor, enthalpy):
    state_now = section(species, cell_scale, diffusivity)
    state_now = section(state_now, cell_scale, diffusivity)
    cell_rows = state_now.reshape(-1, S)
    row_total = cell_rows.shape[0]
    block_size = math.gcd(row_total, 4096)
    order_wide = order_weights.astype(jnp.float32)
    stoich_wide = stoichiometry.astype(jnp.float32)
    advanced_rows, heat_rows = advance(cell_rows, counts.reshape(-1), order_wide, stoich_wide, rate_factor, enthalpy, block_size)
    advanced = advanced_rows.reshape(NX, NY, NZ, S)
    plane_index = (jnp.arange(NZ, dtype=jnp.int32) // CZ)[None, None, :]
    worker_ids = (assignment * N_GZ + plane_index).astype(jnp.int32).reshape(-1)
    totals = jax.ops.segment_sum(heat_rows, worker_ids, num_segments=N_GX * N_GY * N_GZ)
    worker_heat = (totals / CELLS).reshape(N_GX, N_GY, N_GZ)
    return advanced, worker_heat
```

```python
import jax
import jax.numpy as jnp
from jax import lax
from jax.experimental import pallas as pl
from jax.experimental.pallas import tpu as pltpu
from jax.sharding import PartitionSpec as P

MAXSUB = 8
relax_rate = 0.25
AXES = ("gx", "gy", "gz")
MESH = pl.DeviceIdType.MESH


def kernel(
    species,
    counts,
    assignment,
    cell_scale,
    diffusivity,
    order_weights,
    stoichiometry,
    rate_factor,
    enthalpy,
    advanced,
    worker_heat,
    weights_in,
    weights_out,
    weights_tail,
    weights_turned,
    halo_x,
    halo_y,
    halo_z,
    face_z,
    middle,
    rows,
    start_state,
    state,
    rates,
    factors,
    formation,
    cell_counts,
    cell_targets,
    heat_part,
    heat_all,
    load_sem,
    send_sem,
    recv_sem,
    heat_send,
    heat_recv,
):
    spans = [lax.axis_size(axis) for axis in AXES]
    here = [lax.axis_index(axis) for axis in AXES]
    span_y = spans[1]
    group = spans[0] * span_y
    me = here[0] * span_y + here[1]
    cx, cy, cz, width = species.shape
    cells = cx * cy * cz
    depth = order_weights.shape[1]

    loads = [
        pltpu.make_async_copy(order_weights, weights_in, load_sem.at[0]),
        pltpu.make_async_copy(stoichiometry, weights_out, load_sem.at[1]),
    ]
    for load in loads:
        load.start()

    def present(axis_no, side):
        if side == 0:
            return here[axis_no] > 0
        return here[axis_no] < spans[axis_no] - 1

    def peer(offset):
        target = lax.rem(me + offset, group)
        return {"gx": target // span_y, "gy": lax.rem(target, span_y)}

    barrier = pltpu.get_barrier_semaphore()
    for offset in range(1, group):
        pl.semaphore_signal(barrier, inc=1, device_id=peer(offset), device_id_type=MESH)
    for side in range(2):

        @pl.when(present(2, side))
        def _(side=side):
            pl.semaphore_signal(
                barrier, inc=1, device_id={"gz": here[2] + 2 * side - 1}, device_id_type=MESH
            )

    def face_copy(phase, axis_no, side, slot):
        block = species if phase == 0 else middle
        if axis_no == 0:
            source, halo = block.at[0 if side == 0 else cx - 1], halo_x
        elif axis_no == 1:
            source, halo = block.at[:, 0 if side == 0 else cy - 1], halo_y
        else:
            source, halo = face_z.at[phase, side], halo_z
        return pltpu.make_async_remote_copy(
            src_ref=source,
            dst_ref=halo.at[phase, slot],
            send_sem=send_sem.at[phase, axis_no, side],
            recv_sem=recv_sem.at[phase, axis_no, slot],
            device_id={AXES[axis_no]: here[axis_no] + 2 * side - 1},
            device_id_type=MESH,
        )

    def fill_face_z(phase):
        block = species if phase == 0 else middle
        face_z[phase, 0] = block[:, :, 0:1, :]
        face_z[phase, 1] = block[:, :, cz - 1 : cz, :]

    def each_face(action):
        for axis_no in (2, 1, 0):
            for side in range(2):

                @pl.when(present(axis_no, side))
                def _(axis_no=axis_no, side=side):
                    action(axis_no, side)

    fill_face_z(0)
    for phase in range(2):
        for side in range(2):
            for axis_no, halo in enumerate((halo_x, halo_y, halo_z)):

                @pl.when(jnp.logical_not(present(axis_no, side)))
                def _(phase=phase, side=side, halo=halo):
                    halo[phase, side] = jnp.zeros(halo.shape[2:], jnp.float32)

    pl.semaphore_wait(
        barrier,
        group - 1 + present(2, 0).astype(jnp.int32) + present(2, 1).astype(jnp.int32),
    )
    each_face(lambda axis_no, side: face_copy(0, axis_no, side, 1 - side).start())

    rows[...] = jnp.zeros(rows.shape, jnp.float32)
    for source, target in ((counts, cell_counts), (assignment, cell_targets)):
        for x in range(cx):
            for y in range(cy):
                first = x * cy * cz + y * cz
                column = source[y][:, x : x + 1].astype(jnp.float32)
                rows[first : first + cz, :cells] = jnp.broadcast_to(column, (cz, cells))
        target[...] = rows[:, :cells].T[:1]
    padded = rows.shape[1]
    rows[...] = jnp.zeros(rows.shape, jnp.float32)
    rows[:, :width] = jnp.broadcast_to(enthalpy[...].reshape(1, width), (cells, width))
    formation[...] = rows[...].T
    rows[...] = jnp.zeros(rows.shape, jnp.float32)
    factors[...] = jnp.broadcast_to(rate_factor[...].reshape(1, depth), (cells, depth)).T
    spread = diffusivity[...].reshape(1, width)

    def turn_weights():
        loads[0].wait()
        whole = width // 128 * 128
        for first in range(0, whole, 128):
            weights_turned[:, first : first + 128] = weights_in[first : first + 128, :].T
        if whole < width:
            weights_tail[...] = jnp.zeros(weights_tail.shape, jnp.float32)
            weights_tail[: width - whole, :] = weights_in[whole:, :].astype(jnp.float32)
            weights_turned[:, whole : whole + 128] = weights_tail[...].T.astype(jnp.bfloat16)
        if whole + 128 < padded:
            weights_turned[:, whole + 128 :] = jnp.zeros(
                (depth, padded - whole - 128), jnp.bfloat16
            )

    turn_weights()

    def section(phase):
        block = species if phase == 0 else middle
        for x in range(cx):
            low_x = halo_x[phase, 0] if x == 0 else block[x - 1]
            high_x = halo_x[phase, 1] if x == cx - 1 else block[x + 1]
            for y in range(cy):
                now = block[x, y]
                low_y = halo_y[phase, 0, x] if y == 0 else block[x, y - 1]
                high_y = halo_y[phase, 1, x] if y == cy - 1 else block[x, y + 1]
                low_z = jnp.concatenate([halo_z[phase, 0, x, y], now[: cz - 1]], axis=0)
                high_z = jnp.concatenate([now[1:], halo_z[phase, 1, x, y]], axis=0)
                beside = low_x[y] + high_x[y] + low_y + high_y + low_z + high_z
                result = now + cell_scale[y][:, x : x + 1] * spread * (beside - 6.0 * now)
                if phase == 0:
                    middle[x, y] = result
                else:
                    first = x * cy * cz + y * cz
                    rows[first : first + cz, :width] = result

    each_face(lambda axis_no, side: face_copy(0, axis_no, side, side).wait_recv())
    section(0)
    fill_face_z(1)
    each_face(lambda axis_no, side: face_copy(1, axis_no, side, 1 - side).start())
    each_face(lambda axis_no, side: face_copy(1, axis_no, side, side).wait_recv())
    section(1)

    loads[1].wait()
    state[...] = rows[...].T
    start_state[...] = state[...]
    chunk = 256 if depth % 256 == 0 else depth

    def substep(step, carried):
        rounded = state[...].astype(jnp.bfloat16)
        for first in range(0, depth, chunk):
            activity = jnp.dot(
                weights_turned[first : first + chunk, :],
                rounded,
                preferred_element_type=jnp.float32,
            )
            soft = jnp.maximum(activity, 0.0) + jnp.log(1.0 + jnp.exp(-jnp.abs(activity)))
            rates[first : first + chunk, :] = (
                factors[first : first + chunk, :] * soft
            ).astype(jnp.bfloat16)
        change = jnp.dot(weights_out[...], rates[...], preferred_element_type=jnp.float32)
        now = state[:width, :]
        active = cell_counts[...] > step.astype(jnp.float32)
        state[:width, :] = jnp.where(active, now + relax_rate * (change - now), now)
        return carried

    lax.fori_loop(0, MAXSUB, substep, 0)

    released = jnp.sum(
        formation[...] * (start_state[...] - state[...]), axis=0, keepdims=True
    )
    for worker in range(group):
        heat_part[worker] = jnp.where(cell_targets[...] == jnp.float32(worker), released, 0.0)

    def heat_copy(offset):
        return pltpu.make_async_remote_copy(
            src_ref=heat_part.at[lax.rem(me + offset, group)],
            dst_ref=heat_all.at[offset],
            send_sem=heat_send.at[offset],
            recv_sem=heat_recv.at[offset],
            device_id=peer(offset),
            device_id_type=MESH,
        )

    for offset in range(1, group):
        heat_copy(offset).start()

    rows[...] = state[...].T
    for x in range(cx):
        for y in range(cy):
            first = x * cy * cz + y * cz
            advanced[x, y] = rows[first : first + cz, :width]

    total = heat_part[me]
    for offset in range(1, group):
        heat_copy(offset).wait_recv()
        total = total + heat_all[offset]
    worker_heat[0] = jnp.sum(total, axis=1, keepdims=True) / cells

    for phase in range(2):
        each_face(
            lambda axis_no, side, phase=phase: face_copy(
                phase, axis_no, side, 1 - side
            ).wait_send()
        )
    for offset in range(1, group):
        heat_copy(offset).wait_send()


def local(
    species,
    counts,
    assignment,
    cell_scale,
    diffusivity,
    order_weights,
    stoichiometry,
    rate_factor,
    enthalpy,
):
    group = lax.axis_size("gx") * lax.axis_size("gy")
    cx, cy, cz, width = species.shape
    cells = cx * cy * cz
    depth = order_weights.shape[1]
    padded = -(-width // 256) * 256
    vmem = pl.BlockSpec(memory_space=pltpu.VMEM)
    hbm = pl.BlockSpec(memory_space=pltpu.HBM)
    single = jnp.float32
    flops = 4 * MAXSUB * cells * width * depth
    return pl.pallas_call(
        kernel,
        out_shape=(
            jax.ShapeDtypeStruct(species.shape, single),
            jax.ShapeDtypeStruct((1, 1, 1), single),
        ),
        in_specs=[vmem, vmem, vmem, vmem, vmem, hbm, hbm, vmem, vmem],
        out_specs=(vmem, vmem),
        scratch_shapes=[
            pltpu.VMEM(order_weights.shape, jnp.bfloat16),
            pltpu.VMEM(stoichiometry.shape[::-1], jnp.bfloat16),
            pltpu.VMEM((128, depth), single),
            pltpu.VMEM((depth, padded), jnp.bfloat16),
            pltpu.VMEM((2, 2, cy, cz, width), single),
            pltpu.VMEM((2, 2, cx, cz, width), single),
            pltpu.VMEM((2, 2, cx, cy, 1, width), single),
            pltpu.VMEM((2, 2, cx, cy, 1, width), single),
            pltpu.VMEM(species.shape, single),
            pltpu.VMEM((cells, padded), single),
            pltpu.VMEM((padded, cells), single),
            pltpu.VMEM((padded, cells), single),
            pltpu.VMEM((depth, cells), jnp.bfloat16),
            pltpu.VMEM((depth, cells), single),
            pltpu.VMEM((padded, cells), single),
            pltpu.VMEM((1, cells), single),
            pltpu.VMEM((1, cells), single),
            pltpu.VMEM((group, 1, cells), single),
            pltpu.VMEM((group, 1, cells), single),
            pltpu.SemaphoreType.DMA((2,)),
            pltpu.SemaphoreType.DMA((2, 3, 2)),
            pltpu.SemaphoreType.DMA((2, 3, 2)),
            pltpu.SemaphoreType.DMA((group,)),
            pltpu.SemaphoreType.DMA((group,)),
        ],
        compiler_params=pltpu.CompilerParams(
            collective_id=0, has_side_effects=True, vmem_limit_bytes=48 * 1024 * 1024
        ),
        cost_estimate=pl.CostEstimate(
            flops=flops, bytes_accessed=5_000_000, transcendentals=2 * MAXSUB * cells * depth
        ),
    )(
        species,
        counts.transpose(1, 2, 0),
        assignment.transpose(1, 2, 0),
        cell_scale.transpose(1, 2, 0),
        diffusivity,
        order_weights,
        stoichiometry.T,
        rate_factor,
        enthalpy,
    )


def solution(mesh):
    placed = (
        P("gx", "gy", "gz", None),
        P("gx", "gy", "gz"),
        P("gx", "gy", "gz"),
        P("gx", "gy", "gz"),
        P(),
        P(),
        P(),
        P(),
        P(),
    )
    return jax.shard_map(
        local,
        mesh=mesh,
        in_specs=placed,
        out_specs=(P("gx", "gy", "gz", None), P("gx", "gy", "gz")),
        check_vma=False,
    )
```

```python
import jax
import jax.numpy as jnp
from jax import lax
from jax.experimental import pallas as pl
from jax.experimental.pallas import tpu as pltpu
from jax.sharding import PartitionSpec as P

MAXSUB = 8
relax_rate = 0.25
AXES = ("gx", "gy", "gz")
MESH = pl.DeviceIdType.MESH


def kernel(*refs):
    operands, refs = refs[:9], refs[9:]
    (
        advanced,
        worker_heat,
        *held,
        weights_in,
        weights_out,
        weights_tail,
        weights_turned,
        halo_x,
        halo_y,
        halo_z,
        face_z,
        middle,
        rows,
        start_state,
        state,
        rates,
        factors,
        formation,
        cell_counts,
        cell_targets,
        heat_part,
        heat_all,
        load_sem,
        send_sem,
        recv_sem,
        heat_send,
        heat_recv,
    ) = refs
    species, counts, assignment, cell_scale, diffusivity, rate_factor, enthalpy = held
    spans = [lax.axis_size(axis) for axis in AXES]
    here = [lax.axis_index(axis) for axis in AXES]
    span_y = spans[1]
    group = spans[0] * span_y
    me = here[0] * span_y + here[1]
    cx, cy, cz, width = species.shape
    cells = cx * cy * cz
    depth = weights_in.shape[1]

    places = (species, counts, assignment, cell_scale, diffusivity, weights_in, weights_out)
    places = places + (rate_factor, enthalpy)
    loads = [
        pltpu.make_async_copy(operand, place, load_sem.at[number])
        for number, (operand, place) in enumerate(zip(operands, places))
    ]
    for number in (0, 1, 2, 3, 4, 5, 7, 8, 6):
        loads[number].start()

    def present(axis_no, side):
        if side == 0:
            return here[axis_no] > 0
        return here[axis_no] < spans[axis_no] - 1

    def peer(offset):
        target = lax.rem(me + offset, group)
        return {"gx": target // span_y, "gy": lax.rem(target, span_y)}

    barrier = pltpu.get_barrier_semaphore()
    for offset in range(1, group):
        pl.semaphore_signal(barrier, inc=1, device_id=peer(offset), device_id_type=MESH)
    for side in range(2):

        @pl.when(present(2, side))
        def _(side=side):
            pl.semaphore_signal(
                barrier, inc=1, device_id={"gz": here[2] + 2 * side - 1}, device_id_type=MESH
            )

    def face_copy(phase, axis_no, side, slot):
        block = species if phase == 0 else middle
        if axis_no == 0:
            source, halo = block.at[0 if side == 0 else cx - 1], halo_x
        elif axis_no == 1:
            source, halo = block.at[:, 0 if side == 0 else cy - 1], halo_y
        else:
            source, halo = face_z.at[phase, side], halo_z
        return pltpu.make_async_remote_copy(
            src_ref=source,
            dst_ref=halo.at[phase, slot],
            send_sem=send_sem.at[phase, axis_no, side],
            recv_sem=recv_sem.at[phase, axis_no, slot],
            device_id={AXES[axis_no]: here[axis_no] + 2 * side - 1},
            device_id_type=MESH,
        )

    def each_face(action, axes=(2, 1, 0)):
        for axis_no in axes:
            for side in range(2):

                @pl.when(present(axis_no, side))
                def _(axis_no=axis_no, side=side):
                    action(axis_no, side)

    for phase in range(2):
        for side in range(2):
            for axis_no, halo in enumerate((halo_x, halo_y, halo_z)):

                @pl.when(jnp.logical_not(present(axis_no, side)))
                def _(phase=phase, side=side, halo=halo):
                    halo[phase, side] = jnp.zeros(halo.shape[2:], jnp.float32)

    pl.semaphore_wait(
        barrier,
        group - 1 + present(2, 0).astype(jnp.int32) + present(2, 1).astype(jnp.int32),
    )
    loads[0].wait()
    for axes in ((1, 0), (2,)):
        if axes == (2,):
            face_z[0, 0] = species[:, :, 0:1, :]
            face_z[0, 1] = species[:, :, cz - 1 : cz, :]
        each_face(lambda axis_no, side: face_copy(0, axis_no, side, 1 - side).start(), axes)

    padded = rows.shape[1]
    rows[...] = jnp.zeros(rows.shape, jnp.float32)
    for number in range(1, 5):
        loads[number].wait()
    for source, target in ((counts, cell_counts), (assignment, cell_targets)):
        for x in range(cx):
            for y in range(cy):
                first = x * cy * cz + y * cz
                column = source[y][:, x : x + 1].astype(jnp.float32)
                rows[first : first + cz, :cells] = jnp.broadcast_to(column, (cz, cells))
        target[...] = rows[:, :cells].T[:1]
    spread = diffusivity[...].reshape(1, width)

    whole = width // 128 * 128

    def turn_weights(begin, end):
        for first in range(begin, end, 128):
            weights_turned[:, first : first + 128] = weights_in[first : first + 128, :].T

    def turn_tail():
        if whole < width:
            weights_tail[...] = jnp.zeros(weights_tail.shape, jnp.float32)
            weights_tail[: width - whole, :] = weights_in[whole:, :].astype(jnp.float32)
            weights_turned[:, whole : whole + 128] = weights_tail[...].T.astype(jnp.bfloat16)
        if whole + 128 < padded:
            weights_turned[:, whole + 128 :] = jnp.zeros(
                (depth, padded - whole - 128), jnp.bfloat16
            )

    def section(phase, places):
        block = species if phase == 0 else middle
        for x, y in places:
            low_x = halo_x[phase, 0, y] if x == 0 else block[x - 1, y]
            high_x = halo_x[phase, 1, y] if x == cx - 1 else block[x + 1, y]
            now = block[x, y]
            low_y = halo_y[phase, 0, x] if y == 0 else block[x, y - 1]
            high_y = halo_y[phase, 1, x] if y == cy - 1 else block[x, y + 1]
            low_z = jnp.concatenate([halo_z[phase, 0, x, y], now[: cz - 1]], axis=0)
            high_z = jnp.concatenate([now[1:], halo_z[phase, 1, x, y]], axis=0)
            beside = low_x + high_x + low_y + high_y + low_z + high_z
            scale = cell_scale[y][:, x : x + 1]
            result = now + scale * spread * (beside - 6.0 * now)
            if phase == 0:
                middle[x, y] = result
                face_z[1, 0, x, y] = result[:1]
                face_z[1, 1, x, y] = result[cz - 1 :]
            else:
                first = x * cy * cz + y * cz
                rows[first : first + cz, :width] = result

    everywhere = [(x, y) for x in range(cx) for y in range(cy)]
    order = [[], [], []]
    for x, y in everywhere:
        order[0 if x in (0, cx - 1) else 1 if y in (0, cy - 1) else 2].append((x, y))

    halfway = whole // 256 * 128
    loads[5].wait()
    turn_weights(0, halfway)
    each_face(lambda axis_no, side: face_copy(0, axis_no, side, side).wait_recv())
    for axis_no in range(3):
        section(0, order[axis_no])
        each_face(
            lambda axis_no, side: face_copy(1, axis_no, side, 1 - side).start(), (axis_no,)
        )
    turn_weights(halfway, whole)
    turn_tail()
    for number in (7, 8):
        loads[number].wait()
    rows[:, :width] = jnp.broadcast_to(enthalpy[...].reshape(1, width), (cells, width))
    formation[...] = rows[...].T
    factors[...] = jnp.broadcast_to(rate_factor[...].reshape(1, depth), (cells, depth)).T
    each_face(lambda axis_no, side: face_copy(1, axis_no, side, side).wait_recv())
    section(1, everywhere)

    loads[6].wait()
    state[...] = rows[...].T
    start_state[...] = state[...]
    chunk = 256 if depth % 256 == 0 else depth

    def substep(step, carried):
        rounded = state[...].astype(jnp.bfloat16)

        def activities(first):
            return jnp.dot(
                weights_turned[first : first + chunk, :],
                rounded,
                preferred_element_type=jnp.float32,
            )

        activity = activities(0)
        for first in range(0, depth, chunk):
            later = activities(first + chunk) if first + chunk < depth else None
            soft = jnp.maximum(activity, 0.0) + jnp.log(1.0 + jnp.exp(-jnp.abs(activity)))
            rates[first : first + chunk, :] = (
                factors[first : first + chunk, :] * soft
            ).astype(jnp.bfloat16)
            activity = later
        change = jnp.dot(weights_out[...], rates[...], preferred_element_type=jnp.float32)
        now = state[:width, :]
        active = cell_counts[...] > step.astype(jnp.float32)
        state[:width, :] = jnp.where(active, now + relax_rate * (change - now), now)
        return carried

    lax.fori_loop(0, MAXSUB, substep, 0)

    released = jnp.sum(
        formation[...] * (start_state[...] - state[...]), axis=0, keepdims=True
    )
    for worker in range(group):
        heat_part[worker] = jnp.where(cell_targets[...] == jnp.float32(worker), released, 0.0)

    def heat_copy(offset):
        return pltpu.make_async_remote_copy(
            src_ref=heat_part.at[lax.rem(me + offset, group)],
            dst_ref=heat_all.at[offset],
            send_sem=heat_send.at[offset],
            recv_sem=heat_recv.at[offset],
            device_id=peer(offset),
            device_id_type=MESH,
        )

    for offset in range(1, group):
        heat_copy(offset).start()

    rows[...] = state[...].T
    for x in range(cx):
        for y in range(cy):
            first = x * cy * cz + y * cz
            advanced[x, y] = rows[first : first + cz, :width]

    total = heat_part[me]
    for offset in range(1, group):
        heat_copy(offset).wait_recv()
        total = total + heat_all[offset]
    worker_heat[0] = jnp.sum(total, axis=1, keepdims=True) / cells

    for phase in range(2):
        each_face(
            lambda axis_no, side, phase=phase: face_copy(
                phase, axis_no, side, 1 - side
            ).wait_send()
        )
    for offset in range(1, group):
        heat_copy(offset).wait_send()


def local(
    species,
    counts,
    assignment,
    cell_scale,
    diffusivity,
    order_weights,
    stoichiometry,
    rate_factor,
    enthalpy,
):
    group = lax.axis_size("gx") * lax.axis_size("gy")
    cx, cy, cz, width = species.shape
    cells = cx * cy * cz
    depth = order_weights.shape[1]
    padded = -(-width // 256) * 256
    vmem = pl.BlockSpec(memory_space=pltpu.VMEM)
    hbm = pl.BlockSpec(memory_space=pl.ANY)
    single = jnp.float32
    flops = 4 * MAXSUB * cells * width * depth
    return pl.pallas_call(
        kernel,
        out_shape=(
            jax.ShapeDtypeStruct(species.shape, single),
            jax.ShapeDtypeStruct((1, 1, 1), single),
        ),
        in_specs=[hbm] * 9,
        out_specs=(vmem, vmem),
        scratch_shapes=[
            pltpu.VMEM(species.shape, single),
            pltpu.VMEM((cy, cz, cx), counts.dtype),
            pltpu.VMEM((cy, cz, cx), assignment.dtype),
            pltpu.VMEM((cy, cz, cx), single),
            pltpu.VMEM(diffusivity.shape, single),
            pltpu.VMEM(rate_factor.shape, single),
            pltpu.VMEM(enthalpy.shape, single),
            pltpu.VMEM(order_weights.shape, jnp.bfloat16),
            pltpu.VMEM(stoichiometry.shape[::-1], jnp.bfloat16),
            pltpu.VMEM((128, depth), single),
            pltpu.VMEM((depth, padded), jnp.bfloat16),
            pltpu.VMEM((2, 2, cy, cz, width), single),
            pltpu.VMEM((2, 2, cx, cz, width), single),
            pltpu.VMEM((2, 2, cx, cy, 1, width), single),
            pltpu.VMEM((2, 2, cx, cy, 1, width), single),
            pltpu.VMEM(species.shape, single),
            pltpu.VMEM((cells, padded), single),
            pltpu.VMEM((padded, cells), single),
            pltpu.VMEM((padded, cells), single),
            pltpu.VMEM((depth, cells), jnp.bfloat16),
            pltpu.VMEM((depth, cells), single),
            pltpu.VMEM((padded, cells), single),
            pltpu.VMEM((1, cells), single),
            pltpu.VMEM((1, cells), single),
            pltpu.VMEM((group, 1, cells), single),
            pltpu.VMEM((group, 1, cells), single),
            pltpu.SemaphoreType.DMA((9,)),
            pltpu.SemaphoreType.DMA((2, 3, 2)),
            pltpu.SemaphoreType.DMA((2, 3, 2)),
            pltpu.SemaphoreType.DMA((group,)),
            pltpu.SemaphoreType.DMA((group,)),
        ],
        compiler_params=pltpu.CompilerParams(
            collective_id=0, has_side_effects=True, vmem_limit_bytes=63 * 1024 * 1024
        ),
        cost_estimate=pl.CostEstimate(
            flops=flops, bytes_accessed=5_000_000, transcendentals=2 * MAXSUB * cells * depth
        ),
    )(
        species,
        counts.transpose(1, 2, 0),
        assignment.transpose(1, 2, 0),
        cell_scale.transpose(1, 2, 0),
        diffusivity,
        order_weights,
        stoichiometry.T,
        rate_factor,
        enthalpy,
    )


def solution(mesh):
    placed = (
        P("gx", "gy", "gz", None),
        P("gx", "gy", "gz"),
        P("gx", "gy", "gz"),
        P("gx", "gy", "gz"),
        P(),
        P(),
        P(),
        P(),
        P(),
    )
    return jax.shard_map(
        local,
        mesh=mesh,
        in_specs=placed,
        out_specs=(P("gx", "gy", "gz", None), P("gx", "gy", "gz")),
        check_vma=False,
    )
```

```python
import jax
import jax.numpy as jnp
from jax import lax
from jax.experimental import pallas as pl
from jax.experimental.pallas import tpu as pltpu
from jax.sharding import PartitionSpec as P

MAXSUB = 8
relax_rate = 0.25
AXES = ("gx", "gy", "gz")
MESH = pl.DeviceIdType.MESH


def kernel(*refs):
    operands, refs = refs[:9], refs[9:]
    (
        advanced,
        worker_heat,
        *held,
        weights_in,
        weights_out,
        weights_tail,
        weights_turned,
        halo_x,
        halo_y,
        halo_z,
        face_z,
        middle,
        rows,
        start_rows,
        staged,
        cell_counts,
        cell_targets,
        heat_part,
        heat_all,
        load_sem,
        send_sem,
        recv_sem,
        heat_send,
        heat_recv,
    ) = refs
    species, counts, assignment, cell_scale, diffusivity, rate_factor, enthalpy = held
    spans = [lax.axis_size(axis) for axis in AXES]
    here = [lax.axis_index(axis) for axis in AXES]
    span_y = spans[1]
    group = spans[0] * span_y
    me = here[0] * span_y + here[1]
    cx, cy, cz, width = species.shape
    cells = cx * cy * cz
    depth = weights_in.shape[1]

    places = (species, counts, assignment, cell_scale, diffusivity, weights_in, weights_out)
    places = places + (rate_factor, enthalpy)
    loads = [
        pltpu.make_async_copy(operand, place, load_sem.at[number])
        for number, (operand, place) in enumerate(zip(operands, places))
    ]
    for number in (0, 1, 2, 3, 4, 6, 5, 7, 8):
        loads[number].start()

    def present(axis_no, side):
        if side == 0:
            return here[axis_no] > 0
        return here[axis_no] < spans[axis_no] - 1

    def peer(offset):
        target = lax.rem(me + offset, group)
        return {"gx": target // span_y, "gy": lax.rem(target, span_y)}

    barrier = pltpu.get_barrier_semaphore()
    for offset in range(1, group):
        pl.semaphore_signal(barrier, inc=1, device_id=peer(offset), device_id_type=MESH)
    for side in range(2):

        @pl.when(present(2, side))
        def _(side=side):
            pl.semaphore_signal(
                barrier, inc=1, device_id={"gz": here[2] + 2 * side - 1}, device_id_type=MESH
            )

    def face_copy(phase, axis_no, side, slot):
        block = species if phase == 0 else middle
        if axis_no == 0:
            source, halo = block.at[0 if side == 0 else cx - 1], halo_x
        elif axis_no == 1:
            source, halo = block.at[:, 0 if side == 0 else cy - 1], halo_y
        else:
            source, halo = face_z.at[phase, side], halo_z
        return pltpu.make_async_remote_copy(
            src_ref=source,
            dst_ref=halo.at[phase, slot],
            send_sem=send_sem.at[phase, axis_no, side],
            recv_sem=recv_sem.at[phase, axis_no, slot],
            device_id={AXES[axis_no]: here[axis_no] + 2 * side - 1},
            device_id_type=MESH,
        )

    def each_face(action, axes=(2, 1, 0)):
        for axis_no in axes:
            for side in range(2):

                @pl.when(present(axis_no, side))
                def _(axis_no=axis_no, side=side):
                    action(axis_no, side)

    for phase in range(2):
        for side in range(2):
            for axis_no, halo in enumerate((halo_x, halo_y, halo_z)):

                @pl.when(jnp.logical_not(present(axis_no, side)))
                def _(phase=phase, side=side, halo=halo):
                    halo[phase, side] = jnp.zeros(halo.shape[2:], jnp.float32)

    loads[0].wait()
    face_z[0, 0] = species[:, :, 0:1, :]
    face_z[0, 1] = species[:, :, cz - 1 : cz, :]
    pl.semaphore_wait(
        barrier,
        group - 1 + present(2, 0).astype(jnp.int32) + present(2, 1).astype(jnp.int32),
    )
    each_face(lambda axis_no, side: face_copy(0, axis_no, side, 1 - side).start())

    padded = rows.shape[1]
    rows[...] = jnp.zeros(rows.shape, jnp.float32)
    for number in range(1, 5):
        loads[number].wait()
    for source, target in ((counts, cell_counts), (assignment, cell_targets)):
        for x in range(cx):
            for y in range(cy):
                first = x * cy * cz + y * cz
                column = source[y][:, x : x + 1].astype(jnp.float32)
                target[first : first + cz, :] = jnp.broadcast_to(column, (cz, target.shape[1]))
    spread = diffusivity[...].reshape(1, width)

    whole = width // 128 * 128

    def turn_weights(begin, end):
        for first in range(begin, end, 128):
            weights_turned[:, first : first + 128] = weights_out[first : first + 128, :].T

    def turn_tail():
        if whole < width:
            weights_tail[...] = jnp.zeros(weights_tail.shape, jnp.float32)
            weights_tail[: width - whole, :] = weights_out[whole:, :].astype(jnp.float32)
            weights_turned[:, whole : whole + 128] = weights_tail[...].T.astype(jnp.bfloat16)
        if whole + 128 < padded:
            weights_turned[:, whole + 128 :] = jnp.zeros(
                (depth, padded - whole - 128), jnp.bfloat16
            )

    def section(phase, places):
        block = species if phase == 0 else middle
        for x, y in places:
            low_x = halo_x[phase, 0, y] if x == 0 else block[x - 1, y]
            high_x = halo_x[phase, 1, y] if x == cx - 1 else block[x + 1, y]
            now = block[x, y]
            low_y = halo_y[phase, 0, x] if y == 0 else block[x, y - 1]
            high_y = halo_y[phase, 1, x] if y == cy - 1 else block[x, y + 1]
            low_z = jnp.concatenate([halo_z[phase, 0, x, y], now[: cz - 1]], axis=0)
            high_z = jnp.concatenate([now[1:], halo_z[phase, 1, x, y]], axis=0)
            beside = low_x + high_x + low_y + high_y + low_z + high_z
            scale = cell_scale[y][:, x : x + 1]
            result = now + scale * spread * (beside - 6.0 * now)
            if phase == 0:
                middle[x, y] = result
                face_z[1, 0, x, y] = result[:1]
                face_z[1, 1, x, y] = result[cz - 1 :]
            else:
                first = x * cy * cz + y * cz
                rows[first : first + cz, :width] = result

    everywhere = [(x, y) for x in range(cx) for y in range(cy)]
    order = [[], [], []]
    for x, y in everywhere:
        order[0 if x in (0, cx - 1) else 1 if y in (0, cy - 1) else 2].append((x, y))

    halfway = whole // 256 * 128
    loads[6].wait()
    turn_weights(0, halfway)
    each_face(lambda axis_no, side: face_copy(0, axis_no, side, side).wait_recv())
    for axis_no in range(3):
        section(0, order[axis_no])
        each_face(
            lambda axis_no, side: face_copy(1, axis_no, side, 1 - side).start(), (axis_no,)
        )
    turn_weights(halfway, whole)
    turn_tail()
    for number in (5, 7, 8):
        loads[number].wait()
    factors = rate_factor[...].reshape(1, depth)
    each_face(lambda axis_no, side: face_copy(1, axis_no, side, side).wait_recv())
    section(1, everywhere)

    start_rows[...] = rows[...]
    chunk = 256 if depth % 256 == 0 else depth

    def substep(step, carried):
        rounded = rows[:, :width].astype(jnp.bfloat16)

        def activities(first):
            return jnp.dot(
                rounded,
                weights_in[:, first : first + chunk],
                preferred_element_type=jnp.float32,
            )

        change = jnp.zeros((cells, padded), jnp.float32)
        activity = activities(0)
        for first in range(0, depth, chunk):
            later = activities(first + chunk) if first + chunk < depth else None
            soft = jnp.maximum(activity, 0.0) + jnp.log(1.0 + jnp.exp(-jnp.abs(activity)))
            rate_values = (factors[:, first : first + chunk] * soft).astype(jnp.bfloat16)
            change = change + jnp.dot(
                rate_values,
                weights_turned[first : first + chunk, :],
                preferred_element_type=jnp.float32,
            )
            activity = later
        now = rows[...]
        active = cell_counts[:, 0:1] > step.astype(jnp.float32)
        rows[...] = jnp.where(active, now + relax_rate * (change - now), now)
        return carried

    lax.fori_loop(0, MAXSUB, substep, 0)

    released = jnp.sum(
        enthalpy[...].reshape(1, width) * (start_rows[:, :width] - rows[:, :width]),
        axis=1,
        keepdims=True,
    )
    lanes = heat_part.shape[1]
    worker = lax.broadcasted_iota(jnp.int32, (cells, lanes), 1).astype(jnp.float32)
    heat_part[...] = jnp.sum(
        jnp.where(cell_targets[...] == worker, released, 0.0), axis=0, keepdims=True
    )

    def heat_copy(offset):
        return pltpu.make_async_remote_copy(
            src_ref=heat_part,
            dst_ref=heat_all.at[offset],
            send_sem=heat_send.at[offset],
            recv_sem=heat_recv.at[offset],
            device_id=peer(offset),
            device_id_type=MESH,
        )

    for offset in range(1, group):
        heat_copy(offset).start()

    for x in range(cx):
        for y in range(cy):
            first = x * cy * cz + y * cz
            staged[x, y] = rows[first : first + cz, :width]
    leave = pltpu.make_async_copy(staged, advanced, load_sem.at[9])
    leave.start()

    total = heat_part[...]
    for offset in range(1, group):
        heat_copy(offset).wait_recv()
        total = total + heat_all[offset]
    mine = lax.broadcasted_iota(jnp.int32, (1, lanes), 1) == me
    worker_heat[0] = jnp.sum(jnp.where(mine, total, 0.0), axis=1, keepdims=True) / cells
    leave.wait()

    for phase in range(2):
        each_face(
            lambda axis_no, side, phase=phase: face_copy(
                phase, axis_no, side, 1 - side
            ).wait_send()
        )
    for offset in range(1, group):
        heat_copy(offset).wait_send()


def hand_on(block, result, done):
    copies = [
        pltpu.make_async_copy(block.at[x], result.at[x], done.at[x]) for x in range(block.shape[0])
    ]
    for copy in copies:
        copy.start()
    for copy in copies:
        copy.wait()


def local(
    species,
    counts,
    assignment,
    cell_scale,
    diffusivity,
    order_weights,
    stoichiometry,
    rate_factor,
    enthalpy,
):
    group = lax.axis_size("gx") * lax.axis_size("gy")
    cx, cy, cz, width = species.shape
    cells = cx * cy * cz
    depth = order_weights.shape[1]
    padded = -(-width // 256) * 256
    lanes = -(-group // 128) * 128
    vmem = pl.BlockSpec(memory_space=pltpu.VMEM)
    hbm = pl.BlockSpec(memory_space=pl.ANY)
    single = jnp.float32
    flops = 4 * MAXSUB * cells * width * depth
    advanced, worker_heat = pl.pallas_call(
        kernel,
        out_shape=(
            jax.ShapeDtypeStruct(species.shape, single),
            jax.ShapeDtypeStruct((1, 1, 1), single),
        ),
        in_specs=[hbm] * 9,
        out_specs=(hbm, vmem),
        scratch_shapes=[
            pltpu.VMEM(species.shape, single),
            pltpu.VMEM((cy, cz, cx), counts.dtype),
            pltpu.VMEM((cy, cz, cx), assignment.dtype),
            pltpu.VMEM((cy, cz, cx), single),
            pltpu.VMEM(diffusivity.shape, single),
            pltpu.VMEM(rate_factor.shape, single),
            pltpu.VMEM(enthalpy.shape, single),
            pltpu.VMEM(order_weights.shape, jnp.bfloat16),
            pltpu.VMEM(stoichiometry.shape[::-1], jnp.bfloat16),
            pltpu.VMEM((128, depth), single),
            pltpu.VMEM((depth, padded), jnp.bfloat16),
            pltpu.VMEM((2, 2, cy, cz, width), single),
            pltpu.VMEM((2, 2, cx, cz, width), single),
            pltpu.VMEM((2, 2, cx, cy, 1, width), single),
            pltpu.VMEM((2, 2, cx, cy, 1, width), single),
            pltpu.VMEM(species.shape, single),
            pltpu.VMEM((cells, padded), single),
            pltpu.VMEM((cells, padded), single),
            pltpu.VMEM(species.shape, single),
            pltpu.VMEM((cells, lanes), single),
            pltpu.VMEM((cells, lanes), single),
            pltpu.VMEM((1, lanes), single),
            pltpu.VMEM((group, 1, lanes), single),
            pltpu.SemaphoreType.DMA((10,)),
            pltpu.SemaphoreType.DMA((2, 3, 2)),
            pltpu.SemaphoreType.DMA((2, 3, 2)),
            pltpu.SemaphoreType.DMA((group,)),
            pltpu.SemaphoreType.DMA((group,)),
        ],
        compiler_params=pltpu.CompilerParams(
            collective_id=0, has_side_effects=True, vmem_limit_bytes=63 * 1024 * 1024
        ),
        cost_estimate=pl.CostEstimate(
            flops=flops, bytes_accessed=5_000_000, transcendentals=2 * MAXSUB * cells * depth
        ),
    )(
        species,
        counts.transpose(1, 2, 0),
        assignment.transpose(1, 2, 0),
        cell_scale.transpose(1, 2, 0),
        diffusivity,
        order_weights,
        stoichiometry.T,
        rate_factor,
        enthalpy,
    )
    result = pl.pallas_call(
        hand_on,
        out_shape=jax.ShapeDtypeStruct(species.shape, single),
        in_specs=[hbm],
        out_specs=hbm,
        scratch_shapes=[pltpu.SemaphoreType.DMA((cx,))],
        compiler_params=pltpu.CompilerParams(vmem_limit_bytes=63 * 1024 * 1024),
    )(advanced)
    return result, worker_heat


def solution(mesh):
    placed = (
        P("gx", "gy", "gz", None),
        P("gx", "gy", "gz"),
        P("gx", "gy", "gz"),
        P("gx", "gy", "gz"),
        P(),
        P(),
        P(),
        P(),
        P(),
    )
    return jax.shard_map(
        local,
        mesh=mesh,
        in_specs=placed,
        out_specs=(P("gx", "gy", "gz", None), P("gx", "gy", "gz")),
        check_vma=False,
    )
```

```python
import jax
import jax.numpy as jnp
from jax import lax
from jax.experimental import pallas as pl
from jax.experimental.pallas import tpu as pltpu
from jax.sharding import PartitionSpec as P

MAXSUB = 8
relax_rate = 0.25
AXES = ("gx", "gy", "gz")
MESH = pl.DeviceIdType.MESH


def kernel(*refs):
    operands, refs = refs[:9], refs[9:]
    (
        advanced,
        worker_heat,
        *held,
        weights_in,
        weights_out,
        weights_tail,
        weights_turned,
        halo_x,
        halo_y,
        halo_z,
        face_z,
        middle,
        rows,
        start_rows,
        cell_counts,
        cell_targets,
        heat_part,
        heat_all,
        load_sem,
        send_sem,
        recv_sem,
        heat_send,
        heat_recv,
    ) = refs
    species, counts, assignment, cell_scale, diffusivity, rate_factor, enthalpy = held
    spans = [lax.axis_size(axis) for axis in AXES]
    here = [lax.axis_index(axis) for axis in AXES]
    span_y = spans[1]
    group = spans[0] * span_y
    me = here[0] * span_y + here[1]
    cx, cy, cz, width = species.shape
    cells = cx * cy * cz
    depth = weights_in.shape[1]

    places = (species, counts, assignment, cell_scale, diffusivity, weights_in, weights_out)
    places = places + (rate_factor, enthalpy)
    loads = [
        pltpu.make_async_copy(operand, place, load_sem.at[number])
        for number, (operand, place) in enumerate(zip(operands, places))
    ]
    for number in (0, 1, 2, 3, 4, 6, 5, 7, 8):
        loads[number].start()

    def present(axis_no, side):
        if side == 0:
            return here[axis_no] > 0
        return here[axis_no] < spans[axis_no] - 1

    def peer(offset):
        target = lax.rem(me + offset, group)
        return {"gx": target // span_y, "gy": lax.rem(target, span_y)}

    barrier = pltpu.get_barrier_semaphore()
    for offset in range(1, group):
        pl.semaphore_signal(barrier, inc=1, device_id=peer(offset), device_id_type=MESH)
    for side in range(2):

        @pl.when(present(2, side))
        def _(side=side):
            pl.semaphore_signal(
                barrier, inc=1, device_id={"gz": here[2] + 2 * side - 1}, device_id_type=MESH
            )

    def face_copy(phase, axis_no, side, slot):
        block = species if phase == 0 else middle
        if axis_no == 0:
            source, halo = block.at[0 if side == 0 else cx - 1], halo_x
        elif axis_no == 1:
            source, halo = block.at[:, 0 if side == 0 else cy - 1], halo_y
        else:
            source, halo = face_z.at[phase, side], halo_z
        return pltpu.make_async_remote_copy(
            src_ref=source,
            dst_ref=halo.at[phase, slot],
            send_sem=send_sem.at[phase, axis_no, side],
            recv_sem=recv_sem.at[phase, axis_no, slot],
            device_id={AXES[axis_no]: here[axis_no] + 2 * side - 1},
            device_id_type=MESH,
        )

    def each_face(action, axes=(2, 1, 0)):
        for axis_no in axes:
            for side in range(2):

                @pl.when(present(axis_no, side))
                def _(axis_no=axis_no, side=side):
                    action(axis_no, side)

    for phase in range(2):
        for side in range(2):
            for axis_no, halo in enumerate((halo_x, halo_y, halo_z)):

                @pl.when(jnp.logical_not(present(axis_no, side)))
                def _(phase=phase, side=side, halo=halo):
                    halo[phase, side] = jnp.zeros(halo.shape[2:], jnp.float32)

    loads[0].wait()
    face_z[0, 0] = species[:, :, 0:1, :]
    face_z[0, 1] = species[:, :, cz - 1 : cz, :]
    pl.semaphore_wait(
        barrier,
        group - 1 + present(2, 0).astype(jnp.int32) + present(2, 1).astype(jnp.int32),
    )
    each_face(lambda axis_no, side: face_copy(0, axis_no, side, 1 - side).start())

    padded = rows.shape[1]
    rows[...] = jnp.zeros(rows.shape, jnp.float32)
    for number in range(1, 5):
        loads[number].wait()
    for source, target in ((counts, cell_counts), (assignment, cell_targets)):
        for x in range(cx):
            for y in range(cy):
                first = x * cy * cz + y * cz
                column = source[y][:, x : x + 1].astype(jnp.float32)
                target[first : first + cz, :] = jnp.broadcast_to(column, (cz, target.shape[1]))
    spread = diffusivity[...].reshape(1, width)

    whole = width // 128 * 128

    def turn_weights(begin, end):
        for first in range(begin, end, 128):
            weights_turned[:, first : first + 128] = weights_out[first : first + 128, :].T

    def turn_tail():
        if whole < width:
            weights_tail[...] = jnp.zeros(weights_tail.shape, jnp.float32)
            weights_tail[: width - whole, :] = weights_out[whole:, :].astype(jnp.float32)
            weights_turned[:, whole : whole + 128] = weights_tail[...].T.astype(jnp.bfloat16)
        if whole + 128 < padded:
            weights_turned[:, whole + 128 :] = jnp.zeros(
                (depth, padded - whole - 128), jnp.bfloat16
            )

    def section(phase, places):
        block = species if phase == 0 else middle
        for x, y in places:
            low_x = halo_x[phase, 0, y] if x == 0 else block[x - 1, y]
            high_x = halo_x[phase, 1, y] if x == cx - 1 else block[x + 1, y]
            now = block[x, y]
            low_y = halo_y[phase, 0, x] if y == 0 else block[x, y - 1]
            high_y = halo_y[phase, 1, x] if y == cy - 1 else block[x, y + 1]
            low_z = jnp.concatenate([halo_z[phase, 0, x, y], now[: cz - 1]], axis=0)
            high_z = jnp.concatenate([now[1:], halo_z[phase, 1, x, y]], axis=0)
            beside = low_x + high_x + low_y + high_y + low_z + high_z
            scale = cell_scale[y][:, x : x + 1]
            result = now + scale * spread * (beside - 6.0 * now)
            if phase == 0:
                middle[x, y] = result
                face_z[1, 0, x, y] = result[:1]
                face_z[1, 1, x, y] = result[cz - 1 :]
            else:
                first = x * cy * cz + y * cz
                rows[first : first + cz, :width] = result

    everywhere = [(x, y) for x in range(cx) for y in range(cy)]
    order = [[], [], []]
    for x, y in everywhere:
        order[0 if x in (0, cx - 1) else 1 if y in (0, cy - 1) else 2].append((x, y))

    halfway = whole // 256 * 128
    loads[6].wait()
    turn_weights(0, halfway)
    each_face(lambda axis_no, side: face_copy(0, axis_no, side, side).wait_recv())
    for axis_no in range(3):
        section(0, order[axis_no])
        each_face(
            lambda axis_no, side: face_copy(1, axis_no, side, 1 - side).start(), (axis_no,)
        )
    turn_weights(halfway, whole)
    turn_tail()
    for number in (5, 7, 8):
        loads[number].wait()
    factors = rate_factor[...].reshape(1, depth)
    each_face(lambda axis_no, side: face_copy(1, axis_no, side, side).wait_recv())
    section(1, everywhere)

    start_rows[...] = rows[...]
    chunk = 256 if depth % 256 == 0 else depth

    def substep(step, carried):
        rounded = rows[:, :width].astype(jnp.bfloat16)

        def activities(first):
            return jnp.dot(
                rounded,
                weights_in[:, first : first + chunk],
                preferred_element_type=jnp.float32,
            )

        change = jnp.zeros((cells, padded), jnp.float32)
        activity = activities(0)
        for first in range(0, depth, chunk):
            later = activities(first + chunk) if first + chunk < depth else None
            soft = jnp.maximum(activity, 0.0) + jnp.log(1.0 + jnp.exp(-jnp.abs(activity)))
            rate_values = (factors[:, first : first + chunk] * soft).astype(jnp.bfloat16)
            change = change + jnp.dot(
                rate_values,
                weights_turned[first : first + chunk, :],
                preferred_element_type=jnp.float32,
            )
            activity = later
        now = rows[...]
        active = cell_counts[:, 0:1] > step.astype(jnp.float32)
        rows[...] = jnp.where(active, now + relax_rate * (change - now), now)
        return carried

    lax.fori_loop(0, MAXSUB, substep, 0)

    released = jnp.sum(
        enthalpy[...].reshape(1, width) * (start_rows[:, :width] - rows[:, :width]),
        axis=1,
        keepdims=True,
    )
    lanes = heat_part.shape[1]
    worker = lax.broadcasted_iota(jnp.int32, (cells, lanes), 1).astype(jnp.float32)
    heat_part[...] = jnp.sum(
        jnp.where(cell_targets[...] == worker, released, 0.0), axis=0, keepdims=True
    )

    def heat_copy(offset):
        return pltpu.make_async_remote_copy(
            src_ref=heat_part,
            dst_ref=heat_all.at[offset],
            send_sem=heat_send.at[offset],
            recv_sem=heat_recv.at[offset],
            device_id=peer(offset),
            device_id_type=MESH,
        )

    for offset in range(1, group):
        heat_copy(offset).start()

    for x in range(cx):
        for y in range(cy):
            first = x * cy * cz + y * cz
            advanced[x, y] = rows[first : first + cz, :width]

    total = heat_part[...]
    for offset in range(1, group):
        heat_copy(offset).wait_recv()
        total = total + heat_all[offset]
    mine = lax.broadcasted_iota(jnp.int32, (1, lanes), 1) == me
    worker_heat[0] = jnp.sum(jnp.where(mine, total, 0.0), axis=1, keepdims=True) / cells

    for phase in range(2):
        each_face(
            lambda axis_no, side, phase=phase: face_copy(
                phase, axis_no, side, 1 - side
            ).wait_send()
        )
    for offset in range(1, group):
        heat_copy(offset).wait_send()


def local(
    species,
    counts,
    assignment,
    cell_scale,
    diffusivity,
    order_weights,
    stoichiometry,
    rate_factor,
    enthalpy,
):
    group = lax.axis_size("gx") * lax.axis_size("gy")
    cx, cy, cz, width = species.shape
    cells = cx * cy * cz
    depth = order_weights.shape[1]
    padded = -(-width // 256) * 256
    lanes = -(-group // 128) * 128
    vmem = pl.BlockSpec(memory_space=pltpu.VMEM)
    hbm = pl.BlockSpec(memory_space=pl.ANY)
    single = jnp.float32
    flops = 4 * MAXSUB * cells * width * depth
    return pl.pallas_call(
        kernel,
        out_shape=(
            jax.ShapeDtypeStruct(species.shape, single),
            jax.ShapeDtypeStruct((1, 1, 1), single),
        ),
        in_specs=[hbm] * 9,
        out_specs=(vmem, vmem),
        scratch_shapes=[
            pltpu.VMEM(species.shape, single),
            pltpu.VMEM((cy, cz, cx), counts.dtype),
            pltpu.VMEM((cy, cz, cx), assignment.dtype),
            pltpu.VMEM((cy, cz, cx), single),
            pltpu.VMEM(diffusivity.shape, single),
            pltpu.VMEM(rate_factor.shape, single),
            pltpu.VMEM(enthalpy.shape, single),
            pltpu.VMEM(order_weights.shape, jnp.bfloat16),
            pltpu.VMEM(stoichiometry.shape[::-1], jnp.bfloat16),
            pltpu.VMEM((128, depth), single),
            pltpu.VMEM((depth, padded), jnp.bfloat16),
            pltpu.VMEM((2, 2, cy, cz, width), single),
            pltpu.VMEM((2, 2, cx, cz, width), single),
            pltpu.VMEM((2, 2, cx, cy, 1, width), single),
            pltpu.VMEM((2, 2, cx, cy, 1, width), single),
            pltpu.VMEM(species.shape, single),
            pltpu.VMEM((cells, padded), single),
            pltpu.VMEM((cells, padded), single),
            pltpu.VMEM((cells, lanes), single),
            pltpu.VMEM((cells, lanes), single),
            pltpu.VMEM((1, lanes), single),
            pltpu.VMEM((group, 1, lanes), single),
            pltpu.SemaphoreType.DMA((9,)),
            pltpu.SemaphoreType.DMA((2, 3, 2)),
            pltpu.SemaphoreType.DMA((2, 3, 2)),
            pltpu.SemaphoreType.DMA((group,)),
            pltpu.SemaphoreType.DMA((group,)),
        ],
        compiler_params=pltpu.CompilerParams(
            collective_id=0, has_side_effects=True, vmem_limit_bytes=48 * 1024 * 1024
        ),
        cost_estimate=pl.CostEstimate(
            flops=flops, bytes_accessed=5_000_000, transcendentals=2 * MAXSUB * cells * depth
        ),
    )(
        *(
            pltpu.with_memory_space_constraint(operand, pltpu.HBM)
            for operand in (
                species,
                counts.transpose(1, 2, 0),
                assignment.transpose(1, 2, 0),
                cell_scale.transpose(1, 2, 0),
                diffusivity,
                order_weights,
                stoichiometry.T,
                rate_factor,
                enthalpy,
            )
        )
    )


def solution(mesh):
    placed = (
        P("gx", "gy", "gz", None),
        P("gx", "gy", "gz"),
        P("gx", "gy", "gz"),
        P("gx", "gy", "gz"),
        P(),
        P(),
        P(),
        P(),
        P(),
    )
    return jax.shard_map(
        local,
        mesh=mesh,
        in_specs=placed,
        out_specs=(P("gx", "gy", "gz", None), P("gx", "gy", "gz")),
        check_vma=False,
    )
```

```python
import jax
import jax.numpy as jnp
from jax import lax
from jax.experimental import pallas as pl
from jax.experimental.pallas import tpu as pltpu
from jax.sharding import PartitionSpec as P

MAXSUB = 8
relax_rate = 0.25
AXES = ("gx", "gy", "gz")
MESH = pl.DeviceIdType.MESH


def kernel(*refs):
    operands, refs = refs[:9], refs[9:]
    (
        advanced,
        worker_heat,
        *held,
        weights_in,
        weights_out,
        weights_tail,
        weights_turned,
        halo_x,
        halo_y,
        halo_z,
        face_z,
        middle,
        rows,
        start_rows,
        cell_counts,
        cell_targets,
        heat_part,
        heat_all,
        load_sem,
        send_sem,
        recv_sem,
        heat_send,
        heat_recv,
    ) = refs
    species, counts, assignment, cell_scale, diffusivity, rate_factor, enthalpy = held
    spans = [lax.axis_size(axis) for axis in AXES]
    here = [lax.axis_index(axis) for axis in AXES]
    span_y = spans[1]
    group = spans[0] * span_y
    me = here[0] * span_y + here[1]
    cx, cy, cz, width = species.shape
    cells = cx * cy * cz
    depth = weights_in.shape[1]

    places = (species, counts, assignment, cell_scale, diffusivity, weights_in, weights_out)
    places = places + (rate_factor, enthalpy)
    loads = [
        pltpu.make_async_copy(operand, place, load_sem.at[number])
        for number, (operand, place) in enumerate(zip(operands, places))
    ]
    for number in (0, 1, 2, 3, 4, 6, 5, 7, 8):
        loads[number].start()

    def present(axis_no, side):
        if side == 0:
            return here[axis_no] > 0
        return here[axis_no] < spans[axis_no] - 1

    def peer(offset):
        target = lax.rem(me + offset, group)
        return {"gx": target // span_y, "gy": lax.rem(target, span_y)}

    barrier = pltpu.get_barrier_semaphore()
    for offset in range(1, group):
        pl.semaphore_signal(barrier, inc=1, device_id=peer(offset), device_id_type=MESH)
    for side in range(2):

        @pl.when(present(2, side))
        def _(side=side):
            pl.semaphore_signal(
                barrier, inc=1, device_id={"gz": here[2] + 2 * side - 1}, device_id_type=MESH
            )

    def face_copy(phase, axis_no, side, slot):
        block = species if phase == 0 else middle
        if axis_no == 0:
            source, halo = block.at[0 if side == 0 else cx - 1], halo_x
        elif axis_no == 1:
            source, halo = block.at[:, 0 if side == 0 else cy - 1], halo_y
        else:
            source, halo = face_z.at[phase, side], halo_z
        return pltpu.make_async_remote_copy(
            src_ref=source,
            dst_ref=halo.at[phase, slot],
            send_sem=send_sem.at[phase, axis_no, side],
            recv_sem=recv_sem.at[phase, axis_no, slot],
            device_id={AXES[axis_no]: here[axis_no] + 2 * side - 1},
            device_id_type=MESH,
        )

    def each_face(action, axes=(2, 1, 0)):
        for axis_no in axes:
            for side in range(2):

                @pl.when(present(axis_no, side))
                def _(axis_no=axis_no, side=side):
                    action(axis_no, side)

    for phase in range(2):
        for side in range(2):
            for axis_no, halo in enumerate((halo_x, halo_y, halo_z)):

                @pl.when(jnp.logical_not(present(axis_no, side)))
                def _(phase=phase, side=side, halo=halo):
                    halo[phase, side] = jnp.zeros(halo.shape[2:], jnp.float32)

    loads[0].wait()
    face_z[0, 0] = species[:, :, 0:1, :]
    face_z[0, 1] = species[:, :, cz - 1 : cz, :]
    pl.semaphore_wait(
        barrier,
        group - 1 + present(2, 0).astype(jnp.int32) + present(2, 1).astype(jnp.int32),
    )
    each_face(lambda axis_no, side: face_copy(0, axis_no, side, 1 - side).start())

    padded = rows.shape[1]
    rows[...] = jnp.zeros(rows.shape, jnp.float32)
    for number in range(1, 5):
        loads[number].wait()
    for source, target in ((counts, cell_counts), (assignment, cell_targets)):
        for x in range(cx):
            for y in range(cy):
                first = x * cy * cz + y * cz
                column = source[y][:, x : x + 1].astype(jnp.float32)
                target[first : first + cz, :] = jnp.broadcast_to(column, (cz, target.shape[1]))
    spread = diffusivity[...].reshape(1, width)

    whole = width // 128 * 128

    def turn_weights(begin, end):
        for first in range(begin, end, 128):
            weights_turned[:, first : first + 128] = weights_out[first : first + 128, :].T

    def turn_tail():
        if whole < width:
            weights_tail[...] = jnp.zeros(weights_tail.shape, jnp.float32)
            weights_tail[: width - whole, :] = weights_out[whole:, :].astype(jnp.float32)
            weights_turned[:, whole : whole + 128] = weights_tail[...].T.astype(jnp.bfloat16)
        if whole + 128 < padded:
            weights_turned[:, whole + 128 :] = jnp.zeros(
                (depth, padded - whole - 128), jnp.bfloat16
            )

    def section(phase, places):
        block = species if phase == 0 else middle
        for x, y in places:
            low_x = halo_x[phase, 0, y] if x == 0 else block[x - 1, y]
            high_x = halo_x[phase, 1, y] if x == cx - 1 else block[x + 1, y]
            now = block[x, y]
            low_y = halo_y[phase, 0, x] if y == 0 else block[x, y - 1]
            high_y = halo_y[phase, 1, x] if y == cy - 1 else block[x, y + 1]
            low_z = jnp.concatenate([halo_z[phase, 0, x, y], now[: cz - 1]], axis=0)
            high_z = jnp.concatenate([now[1:], halo_z[phase, 1, x, y]], axis=0)
            beside = low_x + high_x + low_y + high_y + low_z + high_z
            scale = cell_scale[y][:, x : x + 1]
            result = now + scale * spread * (beside - 6.0 * now)
            if phase == 0:
                middle[x, y] = result
                face_z[1, 0, x, y] = result[:1]
                face_z[1, 1, x, y] = result[cz - 1 :]
            else:
                first = x * cy * cz + y * cz
                rows[first : first + cz, :width] = result

    everywhere = [(x, y) for x in range(cx) for y in range(cy)]
    order = [[], [], []]
    for x, y in everywhere:
        order[0 if x in (0, cx - 1) else 1 if y in (0, cy - 1) else 2].append((x, y))

    halfway = whole // 256 * 128
    loads[6].wait()
    turn_weights(0, halfway)
    each_face(lambda axis_no, side: face_copy(0, axis_no, side, side).wait_recv())
    for axis_no in range(3):
        section(0, order[axis_no])
        each_face(
            lambda axis_no, side: face_copy(1, axis_no, side, 1 - side).start(), (axis_no,)
        )
    turn_weights(halfway, whole)
    turn_tail()
    for number in (5, 7, 8):
        loads[number].wait()
    factors = rate_factor[...].reshape(1, depth)
    each_face(lambda axis_no, side: face_copy(1, axis_no, side, side).wait_recv())
    section(1, everywhere)

    start_rows[...] = rows[...]
    chunk = 256 if depth % 256 == 0 else depth

    def substep(step, carried):
        rounded = rows[:, :width].astype(jnp.bfloat16)

        def activities(first):
            return jnp.dot(
                rounded,
                weights_in[:, first : first + chunk],
                preferred_element_type=jnp.float32,
            )

        parts = []
        activity = activities(0)
        for first in range(0, depth, chunk):
            later = activities(first + chunk) if first + chunk < depth else None
            soft = jnp.maximum(activity, 0.0) + jnp.log(1.0 + jnp.exp(-jnp.abs(activity)))
            parts.append((factors[:, first : first + chunk] * soft).astype(jnp.bfloat16))
            activity = later
        change = jnp.dot(
            jnp.concatenate(parts, axis=1),
            weights_turned[...],
            preferred_element_type=jnp.float32,
        )
        now = rows[...]
        active = cell_counts[:, 0:1] > step.astype(jnp.float32)
        rows[...] = jnp.where(active, now + relax_rate * (change - now), now)
        return carried

    lax.fori_loop(0, MAXSUB, substep, 0)

    released = jnp.sum(
        enthalpy[...].reshape(1, width) * (start_rows[:, :width] - rows[:, :width]),
        axis=1,
        keepdims=True,
    )
    lanes = heat_part.shape[1]
    worker = lax.broadcasted_iota(jnp.int32, (cells, lanes), 1).astype(jnp.float32)
    heat_part[...] = jnp.sum(
        jnp.where(cell_targets[...] == worker, released, 0.0), axis=0, keepdims=True
    )

    def heat_copy(offset):
        return pltpu.make_async_remote_copy(
            src_ref=heat_part,
            dst_ref=heat_all.at[offset],
            send_sem=heat_send.at[offset],
            recv_sem=heat_recv.at[offset],
            device_id=peer(offset),
            device_id_type=MESH,
        )

    for offset in range(1, group):
        heat_copy(offset).start()

    for x in range(cx):
        for y in range(cy):
            first = x * cy * cz + y * cz
            advanced[x, y] = rows[first : first + cz, :width]

    total = heat_part[...]
    for offset in range(1, group):
        heat_copy(offset).wait_recv()
        total = total + heat_all[offset]
    mine = lax.broadcasted_iota(jnp.int32, (1, lanes), 1) == me
    worker_heat[0] = jnp.sum(jnp.where(mine, total, 0.0), axis=1, keepdims=True) / cells

    for phase in range(2):
        each_face(
            lambda axis_no, side, phase=phase: face_copy(
                phase, axis_no, side, 1 - side
            ).wait_send()
        )
    for offset in range(1, group):
        heat_copy(offset).wait_send()


def local(
    species,
    counts,
    assignment,
    cell_scale,
    diffusivity,
    order_weights,
    stoichiometry,
    rate_factor,
    enthalpy,
):
    group = lax.axis_size("gx") * lax.axis_size("gy")
    cx, cy, cz, width = species.shape
    cells = cx * cy * cz
    depth = order_weights.shape[1]
    padded = -(-width // 256) * 256
    lanes = -(-group // 128) * 128
    vmem = pl.BlockSpec(memory_space=pltpu.VMEM)
    hbm = pl.BlockSpec(memory_space=pl.ANY)
    single = jnp.float32
    flops = 4 * MAXSUB * cells * width * depth
    return pl.pallas_call(
        kernel,
        out_shape=(
            jax.ShapeDtypeStruct(species.shape, single),
            jax.ShapeDtypeStruct((1, 1, 1), single),
        ),
        in_specs=[hbm] * 9,
        out_specs=(vmem, vmem),
        scratch_shapes=[
            pltpu.VMEM(species.shape, single),
            pltpu.VMEM((cy, cz, cx), counts.dtype),
            pltpu.VMEM((cy, cz, cx), assignment.dtype),
            pltpu.VMEM((cy, cz, cx), single),
            pltpu.VMEM(diffusivity.shape, single),
            pltpu.VMEM(rate_factor.shape, single),
            pltpu.VMEM(enthalpy.shape, single),
            pltpu.VMEM(order_weights.shape, jnp.bfloat16),
            pltpu.VMEM(stoichiometry.shape[::-1], jnp.bfloat16),
            pltpu.VMEM((128, depth), single),
            pltpu.VMEM((depth, padded), jnp.bfloat16),
            pltpu.VMEM((2, 2, cy, cz, width), single),
            pltpu.VMEM((2, 2, cx, cz, width), single),
            pltpu.VMEM((2, 2, cx, cy, 1, width), single),
            pltpu.VMEM((2, 2, cx, cy, 1, width), single),
            pltpu.VMEM(species.shape, single),
            pltpu.VMEM((cells, padded), single),
            pltpu.VMEM((cells, padded), single),
            pltpu.VMEM((cells, lanes), single),
            pltpu.VMEM((cells, lanes), single),
            pltpu.VMEM((1, lanes), single),
            pltpu.VMEM((group, 1, lanes), single),
            pltpu.SemaphoreType.DMA((9,)),
            pltpu.SemaphoreType.DMA((2, 3, 2)),
            pltpu.SemaphoreType.DMA((2, 3, 2)),
            pltpu.SemaphoreType.DMA((group,)),
            pltpu.SemaphoreType.DMA((group,)),
        ],
        compiler_params=pltpu.CompilerParams(
            collective_id=0, has_side_effects=True, vmem_limit_bytes=48 * 1024 * 1024
        ),
        cost_estimate=pl.CostEstimate(
            flops=flops, bytes_accessed=5_000_000, transcendentals=2 * MAXSUB * cells * depth
        ),
    )(
        *(
            pltpu.with_memory_space_constraint(operand, pltpu.HBM)
            for operand in (
                species,
                counts.transpose(1, 2, 0),
                assignment.transpose(1, 2, 0),
                cell_scale.transpose(1, 2, 0),
                diffusivity,
                order_weights,
                stoichiometry.T,
                rate_factor,
                enthalpy,
            )
        )
    )


def solution(mesh):
    placed = (
        P("gx", "gy", "gz", None),
        P("gx", "gy", "gz"),
        P("gx", "gy", "gz"),
        P("gx", "gy", "gz"),
        P(),
        P(),
        P(),
        P(),
        P(),
    )
    return jax.shard_map(
        local,
        mesh=mesh,
        in_specs=placed,
        out_specs=(P("gx", "gy", "gz", None), P("gx", "gy", "gz")),
        check_vma=False,
    )
```
